512 devices in a mesh: dp: 64 (over z_lo, x, y), tensor: 8 (over z_hi, core).
Axes of the slice: x: 4, y: 4, z: 16 (z_hi: 4, z_lo: 4; z = z_hi * 4 + z_lo), core: 2. Of those that a mesh axis runs over, the one named last changes fastest.
Arguments:
- tokens: bfloat16 [16384, 8192], P('dp', 'tensor'), may hold values from -6 to 6
- frozen: bfloat16 [1024, 8192], P('dp', 'tensor'), may hold values from -1 to 1
- down_factor: bfloat16 [32, 8192], P(None, 'tensor'), may hold values from -0.125 to 0.125
- up_factor: bfloat16 [2, 16, 512], replicated, may hold values from -0.75 to 0.75
- magnitude: float32 [1024], replicated, may hold values from 0.5 to 2
- key_value_gradient: bfloat16 [16384, 1024], P(('dp', 'tensor')), may hold values from -6 to 6
Outputs:
- projected: bfloat16 [16384, 1024], P(('dp', 'tensor'))
- token_gradient: bfloat16 [16384, 8192], P('dp', 'tensor')
- down_factor_gradient: float32 [32, 8192], P(None, 'tensor')
- up_factor_gradient: float32 [2, 16, 512], replicated
- magnitude_gradient: float32 [1024], replicated
The draws below stay inside these ranges and needn't reach their ends.
All inputs are finite; a program needn't handle non-finite values.
Results may differ from the reference program's by a relative error of at most 0.0055.
Values may be sent and summed in bfloat16 or wider, within the bound.
A program may use at most 64 MiB of HBM per device.

```python
import math
import jax
import jax.numpy as jnp
from jax import lax

MODEL_WIDTH = 8192
KEY_VALUE_WIDTH = 512
ADAPTER_RANK = 16
TOKENS = 16384


def draw_frozen(key, part):
    key = jax.random.fold_in(key, 11)
    key_base, key_cols, key_rows = jax.random.split(key, 3)
    rows = 2 * KEY_VALUE_WIDTH
    position = jnp.arange(MODEL_WIDTH, dtype=jnp.float32) / MODEL_WIDTH
    base = jnp.clip(jax.random.normal(key_base, (rows, MODEL_WIDTH), jnp.float32), -6.0, 6.0)
    rising = jnp.sqrt(1.0 + 2.0 * position)
    col_scale = jnp.exp(jax.random.uniform(key_cols, (1, MODEL_WIDTH), jnp.float32, jnp.log(0.3), jnp.log(3.0)))
    row_scale = jnp.exp(jax.random.uniform(key_rows, (rows, 1), jnp.float32, jnp.log(0.5), jnp.log(2.0)))
    values = base * col_scale * rising[None, :] * row_scale / (2.0 * jnp.sqrt(jnp.float32(MODEL_WIDTH)))
    return jnp.clip(values, -1.0, 1.0).astype(jnp.bfloat16)


def levels(stream_key, dims, cuts, smallest, largest):
    def one(dim, shards_of):
        draws = jax.random.uniform(jax.random.fold_in(jax.random.fold_in(stream_key, 6), dim), (shards_of,), jnp.float32, smallest / len(cuts), largest / len(cuts))
        return jnp.repeat(jnp.exp(draws), dims[dim] // shards_of).reshape((-1,) + (1,) * (len(dims) - dim - 1))

    gain = one(*cuts[0])
    for cut in cuts[1:]:
        gain = gain * one(*cut)
    return gain


def noise(key, dims, width, most, cuts=(), kind=jnp.bfloat16):
    result = width * jax.random.normal(key, dims, jnp.float32)
    if cuts:
        result = result * levels(key, dims, cuts, -0.22, 0.18)
    return jnp.clip(result, -most, most).astype(kind)


def setup_inputs(seed: int = 0) -> dict:
    keys = jax.random.split(jax.random.key(seed), 7)
    tokens = noise(keys[0], (TOKENS, MODEL_WIDTH), 1.0, 6.0, ((0, 64), (1, 8)))
    frozen = draw_frozen(jax.random.fold_in(keys[6], 71), 0)
    down_factor = noise(keys[2], (2 * ADAPTER_RANK, MODEL_WIDTH), (MODEL_WIDTH // 4) ** -0.5, 0.125, ((1, 8),))
    up_factor = noise(keys[3], (2, ADAPTER_RANK, KEY_VALUE_WIDTH), 0.125, 0.75)
    magnitude = jnp.clip(jnp.exp(jax.random.uniform(keys[4], (2 * KEY_VALUE_WIDTH,), jnp.float32, math.log(0.5), math.log(2.0))), 0.5, 2.0)
    key_value_gradient = noise(keys[5], (TOKENS, 2 * KEY_VALUE_WIDTH), 1.0, 6.0, ((0, 512),))
    return dict(tokens=tokens, frozen=frozen, down_factor=down_factor, up_factor=up_factor, magnitude=magnitude, key_value_gradient=key_value_gradient)


stability_eps = 1e-06

def upward_block(up_factor):
    reduced_rank_update = up_factor.shape[1]
    halfway_columns = up_factor.shape[2]
    zeroed_block = jnp.zeros((reduced_rank_update, halfway_columns), up_factor.dtype)
    top_half = jnp.concatenate([up_factor[0], zeroed_block], axis=1)
    bottom_half = jnp.concatenate([zeroed_block, up_factor[1]], axis=1)
    return jnp.concatenate([top_half, bottom_half], axis=0)

def squared_rows(weight_row_slice, down_factor, up_factor_cols):
    count = weight_row_slice.shape[0]
    step = min(256, count)
    down_wide = down_factor.astype(jnp.float32)
    rows3 = weight_row_slice.reshape(count // step, step, weight_row_slice.shape[1])
    cols3 = up_factor_cols.astype(jnp.float32).reshape(count // step, step, up_factor_cols.shape[1])

    def one_block(pair):
        fixed_weight_rows, down_factor_rows = pair
        combined_weight = fixed_weight_rows.astype(jnp.float32) + jnp.dot(down_factor_rows, down_wide, precision=lax.Precision.HIGHEST)
        return lax.optimization_barrier(jnp.sum(combined_weight * combined_weight, axis=1))
    return lax.map(one_block, (rows3, cols3)).reshape(count)

def reference(tokens, frozen, down_factor, up_factor, magnitude, key_value_gradient):
    upper_factor_block = upward_block(up_factor)
    up_wide = upper_factor_block.astype(jnp.float32)
    column_norm = jnp.sqrt(squared_rows(frozen, down_factor, upper_factor_block.T) + stability_eps)
    reduced_product = jnp.dot(tokens, down_factor.T, preferred_element_type=jnp.float32)
    unscaled = jnp.dot(tokens, frozen.T, preferred_element_type=jnp.float32)
    unscaled = unscaled + jnp.dot(reduced_product, up_wide, precision=lax.Precision.HIGHEST)
    factor = magnitude / column_norm
    projected = (unscaled * factor).astype(jnp.bfloat16)
    scaled_grad = (key_value_gradient.astype(jnp.float32) * factor).astype(jnp.bfloat16)
    reduced_gradient = jnp.dot(scaled_grad, upper_factor_block.T, preferred_element_type=jnp.float32).astype(jnp.bfloat16)
    token_gradient = jnp.dot(scaled_grad, frozen, preferred_element_type=jnp.float32)
    token_gradient = (token_gradient + jnp.dot(reduced_gradient, down_factor, preferred_element_type=jnp.float32)).astype(jnp.bfloat16)
    reciprocal_root = 1.0 / math.sqrt(TOKENS)
    down_factor_gradient = jnp.dot(reduced_gradient.T, tokens, preferred_element_type=jnp.float32) * reciprocal_root
    low_q = reduced_product.astype(jnp.bfloat16)
    complete_up_factor = jnp.dot(low_q.T, scaled_grad, preferred_element_type=jnp.float32)
    up_factor_gradient = jnp.stack([complete_up_factor[:ADAPTER_RANK, :KEY_VALUE_WIDTH], complete_up_factor[ADAPTER_RANK:, KEY_VALUE_WIDTH:]]) * reciprocal_root
    magnitude_gradient = lax.optimization_barrier(jnp.sum(key_value_gradient.astype(jnp.float32) * (unscaled / column_norm), axis=0)) * reciprocal_root
    return (projected, token_gradient, down_factor_gradient, up_factor_gradient, magnitude_gradient)
```

```python
import functools
import math

import jax
import jax.numpy as jnp
from jax import lax
from jax.experimental import pallas as pl
from jax.experimental.pallas import tpu as pltpu
from jax.sharding import PartitionSpec as P

stability_eps = 1e-06
MESH = pl.DeviceIdType.MESH
F32 = jnp.float32
BF16 = jnp.bfloat16
OFFSETS = (0, 3, 1, 2)


def nt(a, b):
    return lax.dot_general(a, b, (((1,), (1,)), ((), ())), preferred_element_type=F32)


def nn(a, b):
    return jnp.dot(a, b, preferred_element_type=F32)


def kernel(
    scale,
    tok,
    fro,
    dwn,
    upf,
    mag,
    kvg,
    proj,
    tg,
    da,
    db,
    mgo,
    weight,
    cot,
    up,
    part,
    grad,
    swap_out,
    swap_in,
    hop_out,
    hop_in,
    norm_t,
    norm_z,
    norm_x,
    norm_y,
    mgrad,
    fac,
    inv,
    gpart,
    gplane,
    gdepth,
    gtens,
    gfull,
    f_send,
    f_recv,
    k_send,
    k_recv,
    n_send,
    nt_recv,
    nz_recv,
    nx_recv,
    ny_recv,
    c_send,
    c_recv,
    g1_send,
    g2_send,
    g3_send,
    g4_send,
    g1_recv,
    g2_recv,
    g3_recv,
    g4_recv,
):
    dp = lax.axis_index("dp")
    t = lax.axis_index("tensor")
    rem = lax.rem
    z, p = lax.div(dp, 16), rem(dp, 16)
    x, y = lax.div(p, 4), rem(p, 4)
    h, c = lax.div(t, 2), rem(t, 2)
    sib = (dp, h * 2 + 1 - c)
    sends = []

    def at(zz, xx, yy):
        return ((zz * 4 + xx) * 4 + yy, t)

    def plane(q):
        return (z * 16 + q, t)

    def tens(hh, cc):
        return (dp, hh * 2 + cc)

    def send(src, dst, ssem, rsem, dev):
        d = pltpu.make_async_remote_copy(
            src_ref=src,
            dst_ref=dst,
            send_sem=ssem,
            recv_sem=rsem,
            device_id=dev,
            device_id_type=MESH,
        )
        d.start()
        sends.append(d)

    def arrived(dst, rsem):
        pltpu.make_async_remote_copy(
            src_ref=dst,
            dst_ref=dst,
            send_sem=f_send.at[0],
            recv_sem=rsem,
            device_id=sib,
            device_id_type=MESH,
        ).wait_recv()

    def spread(buf, own, n, peer, ssem, base, rsem):
        for k in range(1, n):
            send(
                buf.at[own], buf.at[own], ssem.at[base + k - 1], rsem.at[own],
                peer(rem(own + k, n)),
            )

    def collect(buf, own, n, rsem):
        for k in range(1, n):
            q = rem(own + k, n)
            arrived(buf.at[q], rsem.at[q])

    def total(buf, n):
        acc = buf[0].astype(F32)
        for i in range(1, n):
            acc = acc + buf[i].astype(F32)
        return acc

    barrier = pltpu.get_barrier_semaphore()

    def greet(dev):
        pl.semaphore_signal(barrier, inc=1, device_id=dev, device_id_type=MESH)

    for k in range(1, 16):
        greet(plane(rem(p + k, 16)))
    for k in range(1, 4):
        greet(at(rem(z + k, 4), x, y))
    for k in range(1, 8):
        greet((dp, rem(t + k, 8)))
    pl.semaphore_wait(barrier, 25)

    for k in range(1, 4):
        send(fro, weight.at[z, x, y], f_send.at[k - 1], f_recv.at[z], at(rem(z + k, 4), x, y))
    up_h, down_h = rem(h + 1, 4), rem(h + 3, 4)
    fwd = rem(h + 1 + 2 * c, 4)
    bwd = rem(h + 3 + 2 * c, 4)
    far = rem(h + 2, 4)
    send(kvg, cot.at[t], k_send.at[0], k_recv.at[0], tens(up_h, c))
    send(kvg, cot.at[t], k_send.at[1], k_recv.at[1], tens(down_h, c))
    send(kvg, cot.at[t], k_send.at[2], k_recv.at[3], sib)
    weight[z, x, y] = fro[...]
    cot[t] = kvg[...]

    up[...] = jnp.zeros_like(up)
    up[0:16, 0:512] = upf[0]
    up[16:32, 512:1024] = upf[1]
    row = lax.broadcasted_iota(jnp.int32, (16, 1024), 0)
    col = lax.broadcasted_iota(jnp.int32, (16, 1024), 1)
    pick = jnp.where(col == row + dp * 16, 1.0, 0.0).astype(BF16)
    mine = nt(pick, up[...]).astype(BF16)
    merged = fro[...].astype(F32) + nn(mine, dwn[...])
    squares = jnp.sum(merged * merged, axis=1, keepdims=True)
    row = lax.broadcasted_iota(jnp.int32, (16, 128), 0)
    col = lax.broadcasted_iota(jnp.int32, (16, 128), 1)
    line = jnp.sum(
        jnp.where(col == row + rem(dp, 8) * 16, squares, 0.0), axis=0, keepdims=True
    )
    row = lax.broadcasted_iota(jnp.int32, (8, 128), 0)
    norm_t[t] = jnp.where(row == lax.div(dp, 8), line, 0.0)
    spread(norm_t, t, 8, lambda q: (dp, q), n_send, 0, nt_recv)

    def unit(half, i, j):
        return weight.at[pl.ds(0, 2), i, j] if half == 0 else weight.at[pl.ds(2, 2), j, i]

    def piece(half, which, i, j):
        return weight.at[which, i, j] if half == 0 else weight.at[2 + which, j, i]

    def dev(half, i, j):
        return at(z, i, j) if half == 0 else at(z, j, i)

    pos = ((x, y), (y, x))

    def sem(half, group, kind):
        return 4 + half * 20 + group * 4 + kind

    def first(half):
        i, j = pos[half]
        for kind, step in ((0, 1), (1, 3)):
            s = sem(half, 0, kind)
            send(unit(half, i, j), unit(half, i, j), f_send.at[s], f_recv.at[s],
                 dev(half, rem(i + step, 4), j))

    def first_relay(half):
        i, j = pos[half]
        for kind, step in ((0, 1), (1, 3)):
            src = rem(i + 4 - step, 4)
            arrived(unit(half, src, j), f_recv.at[sem(half, 0, kind)])
            s = sem(half, 0, 2 + kind)
            send(piece(half, kind, src, j), piece(half, kind, src, j), f_send.at[s],
                 f_recv.at[s], dev(half, rem(i + step, 4), j))

    def first_done(half):
        i, j = pos[half]
        for kind in range(2):
            arrived(piece(half, kind, rem(i + 2, 4), j), f_recv.at[sem(half, 0, 2 + kind)])

    def second(half, g):
        i, j = pos[half]
        u = rem(i + OFFSETS[g], 4)
        for kind, step in ((0, 1), (1, 3)):
            s = sem(half, 1 + g, kind)
            send(unit(half, u, j), unit(half, u, j), f_send.at[s], f_recv.at[s],
                 dev(half, i, rem(j + step, 4)))

    def second_relay(half, g):
        i, j = pos[half]
        u = rem(i + OFFSETS[g], 4)
        for kind, step in ((0, 1), (1, 3)):
            src = rem(j + 4 - step, 4)
            arrived(unit(half, u, src), f_recv.at[sem(half, 1 + g, kind)])
            s = sem(half, 1 + g, 2 + kind)
            send(piece(half, kind, u, src), piece(half, kind, u, src), f_send.at[s],
                 f_recv.at[s], dev(half, i, rem(j + step, 4)))

    def second_done(half, g):
        i, j = pos[half]
        u = rem(i + OFFSETS[g], 4)
        for kind in range(2):
            arrived(piece(half, kind, u, rem(j + 2, 4)),
                    f_recv.at[sem(half, 1 + g, 2 + kind)])

    for k in range(1, 4):
        q = rem(z + k, 4)
        arrived(weight.at[q, x, y], f_recv.at[q])
    for half in range(2):
        first(half)
    for half in range(2):
        second(half, 0)

    collect(norm_t, t, 8, nt_recv)
    norm_z[z] = total(norm_t, 8)
    spread(norm_z, z, 4, lambda q: at(q, x, y), n_send, 7, nz_recv)

    for half in range(2):
        first_relay(half)
    for half in range(2):
        second(half, 1)
        second(half, 2)

    collect(norm_z, z, 4, nz_recv)
    norm_x[x] = total(norm_z, 4)
    spread(norm_x, x, 4, lambda q: at(z, q, y), n_send, 10, nx_recv)

    for half in range(2):
        second_relay(half, 0)
    for half in range(2):
        first_done(half)
        second(half, 3)

    low = nt(tok[...], dwn[...])
    low_hi = low.astype(BF16)
    low_lo = (low - low_hi.astype(F32)).astype(BF16)
    low_t = nt(dwn[...], tok[...])
    low_t_hi = low_t.astype(BF16)
    low_t_lo = (low_t - low_t_hi.astype(F32)).astype(BF16)

    arrived(cot.at[bwd * 2 + c], k_recv.at[c])
    send(cot.at[bwd * 2 + c], cot.at[bwd * 2 + c], k_send.at[3], k_recv.at[2], tens(fwd, c))
    send(cot.at[bwd * 2 + c], cot.at[bwd * 2 + c], k_send.at[4], k_recv.at[4], sib)

    collect(norm_x, x, 4, nx_recv)
    norm_y[y] = total(norm_x, 4)
    spread(norm_y, y, 4, lambda q: at(z, x, q), n_send, 13, ny_recv)

    arrived(cot.at[fwd * 2 + c], k_recv.at[1 - c])
    send(cot.at[fwd * 2 + c], cot.at[fwd * 2 + c], k_send.at[5], k_recv.at[5], sib)

    for half in range(2):
        second_relay(half, 1)
    for half in range(2):
        second_relay(half, 2)

    collect(norm_y, y, 4, ny_recv)
    norm = jnp.sqrt(total(norm_y, 4) + stability_eps)
    fac[...] = mag[...] / norm
    inv[...] = 1.0 / norm

    for half in range(2):
        second_relay(half, 3)

    arrived(cot.at[far * 2 + c], k_recv.at[2])
    send(cot.at[far * 2 + c], cot.at[far * 2 + c], k_send.at[6], k_recv.at[6], sib)
    arrived(cot.at[h * 2 + 1 - c], k_recv.at[3])
    arrived(cot.at[fwd * 2 + 1 - c], k_recv.at[4])
    arrived(cot.at[bwd * 2 + 1 - c], k_recv.at[5])
    arrived(cot.at[far * 2 + 1 - c], k_recv.at[6])

    for i in range(8):
        cols = pl.ds(i * 128, 128)
        grad[:, cols] = (
            cot[:, :, cols].reshape(256, 128).astype(F32) * fac[i : i + 1, :]
        ).astype(BF16)
    low_grad = nt(grad[...], up[...]).astype(BF16)
    low_grad_t = nt(up[...], grad[...]).astype(BF16)
    grad_a = nn(low_grad_t, tok[...])
    grad_b = nn(low_t_hi, grad[...]) + nn(low_t_lo, grad[...])

    for half in range(2):
        for g in range(4):
            second_done(half, g)

    for j in range(4):
        cols = pl.ds(j * 256, 256)
        rows = weight[j].reshape(256, 1024)
        out = nt(tok[...], rows) + nn(low_hi, up[:, cols]) + nn(low_lo, up[:, cols])
        part[:, :, :, cols] = out.reshape(4, 2, 32, 256)
        swap_out[j] = part[:, 1 - c, :, cols].astype(BF16)
        send(swap_out.at[j], swap_in.at[j], c_send.at[j], c_recv.at[j], sib)
        m = jnp.sum(
            cot[:, :, cols].reshape(256, 256).astype(F32) * out, axis=0, keepdims=True
        )
        mgrad[2 * j : 2 * j + 1, :] = m[:, 0:128]
        mgrad[2 * j + 1 : 2 * j + 2, :] = m[:, 128:256]

    mg = mgrad[...] * inv[...]
    for q in range(16):
        r, b = q // 8, q % 8
        gb = grad_b[8 * r : 8 * r + 8] if b < 4 else grad_b[16 + 8 * r : 24 + 8 * r]
        gpart[q] = jnp.concatenate(
            [
                grad_a[16 * r : 16 * r + 16, 128 * b : 128 * b + 128],
                gb[:, 128 * b : 128 * b + 128],
                jnp.broadcast_to(mg[b : b + 1, :], (8, 128)),
            ],
            axis=0,
        ).astype(BF16)
    for k in range(1, 16):
        q = rem(p + k, 16)
        send(gpart.at[q], gplane.at[p], g1_send.at[k - 1], g1_recv.at[p], plane(q))
    gplane[p] = gpart[p]

    for j in range(4):
        cols = pl.ds(j * 256, 256)
        arrived(swap_in.at[j], c_recv.at[j])
        both = part[:, c, :, cols] + swap_in[j].astype(F32)
        part[:, c, :, cols] = both
        hop_out[j, 0] = part[far, c, :, cols].astype(BF16)
        send(hop_out.at[j, 0], hop_in.at[j, 0], c_send.at[4 + j], c_recv.at[4 + j],
             tens(fwd, c))
        hop_out[j, 1] = part[bwd, c, :, cols].astype(BF16)
        send(hop_out.at[j, 1], hop_in.at[j, 1], c_send.at[8 + j], c_recv.at[8 + j],
             tens(bwd, c))

    for j in range(4):
        cols = pl.ds(j * 256, 256)
        rows = weight[:, :, :, :, cols].reshape(1024, 256)
        tg[:, cols] = (nn(grad[...], rows) + nn(low_grad, dwn[:, cols])).astype(BF16)

    collect(gplane, p, 16, g1_recv)
    gdepth[z] = total(gplane, 16)
    spread(gdepth, z, 4, lambda q: at(q, x, y), g2_send, 0, g2_recv)

    for j in range(4):
        cols = pl.ds(j * 256, 256)
        arrived(hop_in.at[j, 0], c_recv.at[4 + j])
        hop_out[j, 2] = (part[fwd, c, :, cols] + hop_in[j, 0].astype(F32)).astype(BF16)
        send(hop_out.at[j, 2], hop_in.at[j, 2], c_send.at[12 + j], c_recv.at[12 + j],
             tens(fwd, c))

    collect(gdepth, z, 4, g2_recv)
    deep = total(gdepth, 4)
    gtens[t] = deep[16:32]
    spread(gtens, t, 8, lambda q: (dp, q), g3_send, 0, g3_recv)
    collect(gtens, t, 8, g3_recv)
    gfull[p] = jnp.concatenate([deep[0:16], total(gtens, 8)], axis=0).astype(BF16)
    spread(gfull, p, 16, plane, g4_send, 0, g4_recv)

    for j in range(4):
        cols = pl.ds(j * 256, 256)
        arrived(hop_in.at[j, 1], c_recv.at[8 + j])
        arrived(hop_in.at[j, 2], c_recv.at[12 + j])
        summed = (
            part[h, c, :, cols] + hop_in[j, 1].astype(F32) + hop_in[j, 2].astype(F32)
        )
        f = jnp.concatenate([fac[2 * j : 2 * j + 1, :], fac[2 * j + 1 : 2 * j + 2, :]], axis=1)
        proj[:, cols] = (summed * f).astype(BF16)

    collect(gfull, p, 16, g4_recv)
    for q in range(16):
        r, b = q // 8, q % 8
        got = gfull[q].astype(F32) * scale
        da[16 * r : 16 * r + 16, 128 * b : 128 * b + 128] = got[0:16]
        lo = 128 * (b % 4)
        db[b // 4, 8 * r : 8 * r + 8, lo : lo + 128] = got[16:24]
        if r == 0:
            mgo[b : b + 1, :] = got[24:25]

    for d in sends:
        d.wait_send()


def body(tokens, frozen, down_factor, up_factor, magnitude, key_value_gradient):
    scale = 1.0 / math.sqrt(tokens.shape[0] * lax.axis_size("dp"))
    dma = pltpu.SemaphoreType.DMA
    vmem = pl.BlockSpec(memory_space=pltpu.VMEM)
    projected, token_gradient, grad_a, grad_b, grad_m = pl.pallas_call(
        functools.partial(kernel, scale),
        out_shape=(
            jax.ShapeDtypeStruct((32, 1024), BF16),
            jax.ShapeDtypeStruct((256, 1024), BF16),
            jax.ShapeDtypeStruct((32, 1024), F32),
            jax.ShapeDtypeStruct((2, 16, 512), F32),
            jax.ShapeDtypeStruct((8, 128), F32),
        ),
        in_specs=[vmem] * 6,
        out_specs=(vmem,) * 5,
        scratch_shapes=[
            pltpu.VMEM((4, 4, 4, 16, 1024), BF16),
            pltpu.VMEM((8, 32, 1024), BF16),
            pltpu.VMEM((32, 1024), BF16),
            pltpu.VMEM((4, 2, 32, 1024), F32),
            pltpu.VMEM((256, 1024), BF16),
            pltpu.VMEM((4, 4, 32, 256), BF16),
            pltpu.VMEM((4, 4, 32, 256), BF16),
            pltpu.VMEM((4, 3, 32, 256), BF16),
            pltpu.VMEM((4, 3, 32, 256), BF16),
            pltpu.VMEM((8, 8, 128), F32),
            pltpu.VMEM((4, 8, 128), F32),
            pltpu.VMEM((4, 8, 128), F32),
            pltpu.VMEM((4, 8, 128), F32),
            pltpu.VMEM((8, 128), F32),
            pltpu.VMEM((8, 128), F32),
            pltpu.VMEM((8, 128), F32),
            pltpu.VMEM((16, 32, 128), BF16),
            pltpu.VMEM((16, 32, 128), BF16),
            pltpu.VMEM((4, 32, 128), F32),
            pltpu.VMEM((8, 16, 128), F32),
            pltpu.VMEM((16, 32, 128), BF16),
            dma((44,)),
            dma((44,)),
            dma((7,)),
            dma((7,)),
            dma((16,)),
            dma((8,)),
            dma((4,)),
            dma((4,)),
            dma((4,)),
            dma((16,)),
            dma((16,)),
            dma((15,)),
            dma((3,)),
            dma((7,)),
            dma((15,)),
            dma((16,)),
            dma((4,)),
            dma((8,)),
            dma((16,)),
        ],
        compiler_params=pltpu.CompilerParams(
            collective_id=0, has_side_effects=True, vmem_limit_bytes=32 * 1024 * 1024
        ),
        cost_estimate=pl.CostEstimate(
            flops=1200000000, bytes_accessed=2000000, transcendentals=0
        ),
    )(
        tokens,
        frozen,
        down_factor,
        up_factor,
        magnitude.reshape(8, 128),
        key_value_gradient,
    )
    return projected, token_gradient, grad_a, grad_b, grad_m.reshape(1024)


def solution(mesh):
    placed = (
        P("dp", "tensor"),
        P("dp", "tensor"),
        P(None, "tensor"),
        P(),
        P(),
        P(("dp", "tensor"), None),
    )
    return jax.shard_map(
        body,
        mesh=mesh,
        in_specs=placed,
        out_specs=(P(("dp", "tensor"), None), P("dp", "tensor"), P(None, "tensor"), P(), P()),
        check_vma=False,
    )
```

```python
import functools
import math

import jax
import jax.numpy as jnp
from jax import lax
from jax.experimental import pallas as pl
from jax.experimental.pallas import tpu as pltpu
from jax.sharding import PartitionSpec as P

stability_eps = 1e-06
MESH = pl.DeviceIdType.MESH
F32 = jnp.float32
BF16 = jnp.bfloat16
OFFSETS = (0, 3, 1, 2)


def nt(a, b):
    return lax.dot_general(a, b, (((1,), (1,)), ((), ())), preferred_element_type=F32)


def nn(a, b):
    return jnp.dot(a, b, preferred_element_type=F32)


def kernel(
    scale,
    tok_in,
    fro,
    dwn_in,
    upf,
    mag_in,
    kvg,
    proj_out,
    tg_out,
    da_out,
    db_out,
    mg_out,
    proj,
    tg,
    da,
    db,
    mgo,
    tok,
    dwn,
    mag,
    weight,
    cot,
    up,
    part,
    pair,
    grad,
    swap_out,
    swap_in,
    hop_out,
    hop_in,
    norms,
    mags,
    facrow,
    low_swap,
    lows,
    gpart,
    gplane,
    gdepth,
    gfull,
    in_sem,
    out_sem,
    f_send,
    f_recv,
    k_send,
    k_recv,
    n_send,
    n_recv,
    m_send,
    m_recv,
    l_send,
    l_recv,
    c_send,
    c_recv,
    g1_send,
    g2_send,
    g4_send,
    g1_recv,
    g2_recv,
    g4_recv,
):
    dp = lax.axis_index("dp")
    t = lax.axis_index("tensor")
    rem = lax.rem
    z, p = lax.div(dp, 16), rem(dp, 16)
    x, y = lax.div(p, 4), rem(p, 4)
    h, c = lax.div(t, 2), rem(t, 2)
    sib = (dp, h * 2 + 1 - c)
    fwd = rem(h + 1 + 2 * c, 4)
    bwd = rem(h + 3 + 2 * c, 4)
    far = rem(h + 2, 4)
    sends = []
    writes = []

    def at(zz, xx, yy):
        return ((zz * 4 + xx) * 4 + yy, t)

    def plane(q):
        return (z * 16 + q, t)

    def depth(q):
        return at(q, x, y)

    def tens(hh):
        return (dp, hh * 2 + c)

    def send(src, dst, ssem, rsem, dev):
        d = pltpu.make_async_remote_copy(
            src_ref=src,
            dst_ref=dst,
            send_sem=ssem,
            recv_sem=rsem,
            device_id=dev,
            device_id_type=MESH,
        )
        d.start()
        sends.append(d)

    def arrived(dst, rsem):
        pltpu.make_async_remote_copy(
            src_ref=dst,
            dst_ref=dst,
            send_sem=f_send.at[0],
            recv_sem=rsem,
            device_id=sib,
            device_id_type=MESH,
        ).wait_recv()

    def spread(buf, own, n, peer, ssem, rsem, base=0, sbase=0):
        for k in range(1, n):
            send(
                buf.at[base + own], buf.at[base + own], ssem.at[sbase + k - 1],
                rsem.at[base + own], peer(rem(own + k, n)),
            )

    def collect(buf, own, n, rsem, base=0):
        for k in range(1, n):
            q = base + rem(own + k, n)
            arrived(buf.at[q], rsem.at[q])

    def total(buf, n, base=0):
        acc = buf[base].astype(F32)
        for i in range(1, n):
            acc = acc + buf[base + i].astype(F32)
        return acc

    def write(src, dst, i):
        w = pltpu.make_async_copy(src, dst, out_sem.at[i])
        w.start()
        writes.append(w)

    loads = [
        pltpu.make_async_copy(src, dst, in_sem.at[i])
        for i, (src, dst) in enumerate(
            (
                (fro, weight.at[0, x, y]),
                (dwn_in, dwn),
                (upf.at[0], up.at[pl.ds(0, 16), pl.ds(0, 512)]),
                (upf.at[1], up.at[pl.ds(16, 16), pl.ds(512, 512)]),
                (kvg, cot.at[t]),
                (tok_in, tok),
                (mag_in, mag),
            )
        )
    ]
    for load in loads:
        load.start()

    barrier = pltpu.get_barrier_semaphore()

    def greet(dev):
        pl.semaphore_signal(barrier, inc=1, device_id=dev, device_id_type=MESH)

    greet(tens(fwd))
    greet(tens(bwd))
    for k in range(1, 4):
        greet(depth(rem(z + k, 4)))
    for k in range(1, 16):
        greet(plane(rem(p + k, 16)))
    greet(sib)

    class Tile:
        def __init__(self, buf, ssem, rsem):
            self.buf, self.ssem, self.rsem = buf, ssem, rsem

        def core_send(self, value):
            self.buf[c] = value
            send(self.buf.at[c], self.buf.at[c], self.ssem.at[0], self.rsem.at[c], sib)

        def core_sum(self):
            arrived(self.buf.at[1 - c], self.rsem.at[1 - c])
            return self.buf[0] + self.buf[1]

        def ring_send(self, value):
            own = self.buf.at[2 + h]
            own[...] = value
            send(own, own, self.ssem.at[1], self.rsem.at[2 + h], tens(fwd))
            send(own, own, self.ssem.at[2], self.rsem.at[2 + h], tens(bwd))

        def ring_relay(self):
            got = self.buf.at[2 + bwd]
            arrived(got, self.rsem.at[2 + bwd])
            send(got, got, self.ssem.at[3], self.rsem.at[2 + bwd], tens(fwd))

        def ring_sum(self):
            arrived(self.buf.at[2 + fwd], self.rsem.at[2 + fwd])
            arrived(self.buf.at[2 + far], self.rsem.at[2 + far])
            return total(self.buf, 4, 2)

        def depth_send(self, value):
            self.buf[6 + z] = value
            spread(self.buf, z, 4, depth, self.ssem, self.rsem, 6, 4)

        def depth_sum(self):
            collect(self.buf, z, 4, self.rsem, 6)
            return total(self.buf, 4, 6)

        def plane_send(self, value):
            self.buf[10 + p] = value
            spread(self.buf, p, 16, plane, self.ssem, self.rsem, 10, 7)

        def plane_sum(self):
            collect(self.buf, p, 16, self.rsem, 10)
            return total(self.buf, 16, 10)

    norm_tile = Tile(norms, n_send, n_recv)
    mag_tile = Tile(mags, m_send, m_recv)

    up[0:16, 512:1024] = jnp.zeros((16, 512), BF16)
    up[16:32, 0:512] = jnp.zeros((16, 512), BF16)
    for load in loads:
        load.wait()
    row = lax.broadcasted_iota(jnp.int32, (16, 1024), 0)
    col = lax.broadcasted_iota(jnp.int32, (16, 1024), 1)
    pick = jnp.where(col == row + dp * 16, 1.0, 0.0).astype(BF16)
    mine = nt(pick, up[...]).astype(BF16)
    merged = weight[0, x, y].astype(F32) + nn(mine, dwn[...])
    squares = jnp.sum(merged * merged, axis=1, keepdims=True)
    row = lax.broadcasted_iota(jnp.int32, (16, 128), 0)
    col = lax.broadcasted_iota(jnp.int32, (16, 128), 1)
    line = jnp.sum(
        jnp.where(col == row + rem(dp, 8) * 16, squares, 0.0), axis=0, keepdims=True
    )
    row8 = lax.broadcasted_iota(jnp.int32, (8, 128), 0)
    own_squares = jnp.where(row8 == lax.div(dp, 8), line, 0.0)

    pl.semaphore_wait(barrier, 21)

    own_rows = weight.at[0, x, y]
    for k in range(1, 4):
        send(own_rows, weight.at[4 - k, x, y], f_send.at[k], f_recv.at[4 - k],
             depth(rem(z + k, 4)))
    norm_tile.core_send(own_squares)

    slots = (pl.ds(0, 1), pl.ds(1, 3))
    pos = ((x, y), (y, x))

    def block(half, grp, i, j, lo, wide):
        i, j = (i, j) if half == 0 else (j, i)
        return weight.at[slots[grp], i, j, :, pl.ds(half * 512 + lo, wide)]

    def unit(half, grp, i, j):
        return block(half, grp, i, j, 0, 512)

    def piece(half, grp, kind, i, j):
        return block(half, grp, i, j, 256 * kind, 256)

    def peer(half, i, j):
        return at(z, i, j) if half == 0 else at(z, j, i)

    def sem(half, grp, step, kind):
        return 4 + ((half * 2 + grp) * 5 + step) * 4 + kind

    def pass_on(ref, s, dev):
        send(ref, ref, f_send.at[s], f_recv.at[s], dev)

    def first(grp):
        for kind, step in ((0, 1), (1, 3)):
            for half in range(2):
                i, j = pos[half]
                pass_on(unit(half, grp, i, j), sem(half, grp, 0, kind),
                        peer(half, rem(i + step, 4), j))

    def first_relay(grp):
        for kind, step in ((0, 1), (1, 3)):
            for half in range(2):
                i, j = pos[half]
                src = rem(i + 4 - step, 4)
                arrived(unit(half, grp, src, j), f_recv.at[sem(half, grp, 0, kind)])
                pass_on(piece(half, grp, kind, src, j), sem(half, grp, 0, 2 + kind),
                        peer(half, rem(i + step, 4), j))

    def first_done(grp):
        for kind in range(2):
            for half in range(2):
                i, j = pos[half]
                arrived(piece(half, grp, kind, rem(i + 2, 4), j),
                        f_recv.at[sem(half, grp, 0, 2 + kind)])

    def second(grp, g):
        for kind, step in ((0, 1), (1, 3)):
            for half in range(2):
                i, j = pos[half]
                u = rem(i + OFFSETS[g], 4)
                pass_on(unit(half, grp, u, j), sem(half, grp, 1 + g, kind),
                        peer(half, i, rem(j + step, 4)))

    def second_relay(grp, g):
        for kind, step in ((0, 1), (1, 3)):
            for half in range(2):
                i, j = pos[half]
                u, src = rem(i + OFFSETS[g], 4), rem(j + 4 - step, 4)
                arrived(unit(half, grp, u, src), f_recv.at[sem(half, grp, 1 + g, kind)])
                pass_on(piece(half, grp, kind, u, src), sem(half, grp, 1 + g, 2 + kind),
                        peer(half, i, rem(j + step, 4)))

    def second_done(grp, g):
        for kind in range(2):
            for half in range(2):
                i, j = pos[half]
                arrived(piece(half, grp, kind, rem(i + OFFSETS[g], 4), rem(j + 2, 4)),
                        f_recv.at[sem(half, grp, 1 + g, 2 + kind)])

    first(0)
    second(0, 0)

    low = nt(tok[...], dwn[...])
    low_hi = low.astype(BF16)
    low_lo = (low - low_hi.astype(F32)).astype(BF16)
    low_swap[c] = nt(dwn[...], tok[...])
    send(low_swap.at[c], low_swap.at[c], l_send.at[0], l_recv.at[c], sib)

    norm_tile.ring_send(norm_tile.core_sum())

    def cot_at(hh, cc, i):
        return cot.at[hh * 2 + cc, :, pl.ds(256 * i, 256)]

    def cot_send(hh, kind, i, dev):
        ref = cot_at(hh, c, i)
        send(ref, ref, k_send.at[kind * 4 + i], k_recv.at[kind * 4 + i], dev)

    for i in range(4):
        cot_send(h, 0, i, tens(fwd))
    arrived(low_swap.at[1 - c], l_recv.at[1 - c])
    own_low = lows.at[h]
    own_low[...] = (low_swap[0] + low_swap[1]).astype(BF16)
    send(own_low, own_low, l_send.at[1], l_recv.at[2 + h], tens(fwd))
    send(own_low, own_low, l_send.at[2], l_recv.at[2 + h], tens(bwd))
    for i in range(4):
        cot_send(h, 1, i, tens(bwd))
    for i in range(4):
        cot_send(h, 3, i, sib)

    first_relay(0)
    second(0, 1)
    second(0, 2)
    second_relay(0, 0)
    first_done(0)
    second(0, 3)

    for k in range(1, 4):
        arrived(weight.at[k, x, y], f_recv.at[k])
    first(1)
    second(1, 0)
    norm_tile.ring_relay()
    second_relay(0, 1)
    second_relay(0, 2)
    first_relay(1)
    second(1, 1)
    second(1, 2)
    second_relay(0, 3)
    for i in range(4):
        arrived(cot_at(bwd, c, i), k_recv.at[i])
        cot_send(bwd, 2, i, tens(fwd))
        cot_send(bwd, 4, i, sib)
    second_relay(1, 0)
    first_done(1)
    second(1, 3)
    arrived(lows.at[bwd], l_recv.at[2 + bwd])
    send(lows.at[bwd], lows.at[bwd], l_send.at[3], l_recv.at[2 + bwd], tens(fwd))
    norm_tile.depth_send(norm_tile.ring_sum())
    second_relay(1, 1)
    second_relay(1, 2)
    norm_tile.plane_send(norm_tile.depth_sum())
    second_relay(1, 3)
    for i in range(4):
        arrived(cot_at(fwd, c, i), k_recv.at[4 + i])
        cot_send(fwd, 5, i, sib)
    for g in range(4):
        for grp in range(2):
            second_done(grp, g)

    def outputs(k):
        return pl.ds(pl.multiple_of(rem(z + k, 4) * 256, 256), 256)

    for k in range(4):
        cols = outputs(k)
        rows = weight[k].reshape(256, 1024)
        out = nt(tok[...], rows) + nn(low_hi, up[:, cols]) + nn(low_lo, up[:, cols])
        part[k] = out.reshape(4, 2, 32, 256)
        swap_out[k] = part[k, :, 1 - c].astype(BF16)
        send(swap_out.at[k], swap_in.at[k], c_send.at[k], c_recv.at[k], sib)

    for i in range(4):
        arrived(cot_at(far, c, i), k_recv.at[8 + i])
        cot_send(far, 6, i, sib)

    for k in range(4):
        arrived(swap_in.at[k], c_recv.at[k])
        pair[k] = part[k, :, c] + swap_in[k].astype(F32)
        hop_out[k, 0] = pair[k, far].astype(BF16)
        send(hop_out.at[k, 0], hop_in.at[k, 0], c_send.at[4 + k], c_recv.at[4 + k], tens(fwd))
    for k in range(4):
        hop_out[k, 1] = pair[k, bwd].astype(BF16)
        send(hop_out.at[k, 1], hop_in.at[k, 1], c_send.at[8 + k], c_recv.at[8 + k], tens(bwd))

    for i in range(4):
        arrived(cot_at(h, 1 - c, i), k_recv.at[12 + i])
        arrived(cot_at(fwd, 1 - c, i), k_recv.at[16 + i])
        arrived(cot_at(bwd, 1 - c, i), k_recv.at[20 + i])
        arrived(cot_at(far, 1 - c, i), k_recv.at[24 + i])

    mg = jnp.zeros((8, 128), F32)
    for k in range(4):
        m = jnp.sum(
            cot[:, :, outputs(k)].reshape(256, 256).astype(F32) * part[k].reshape(256, 256),
            axis=0,
            keepdims=True,
        )
        r = rem(z + k, 4) * 2
        mg = mg + jnp.where(row8 == r, m[:, 0:128], 0.0)
        mg = mg + jnp.where(row8 == r + 1, m[:, 128:256], 0.0)
    mag_tile.core_send(mg)

    norm = jnp.sqrt(norm_tile.plane_sum() + stability_eps)
    fac = mag[...] / norm
    for i in range(8):
        cols = pl.ds(i * 128, 128)
        facrow[:, cols] = fac[i : i + 1, :]
        grad[:, cols] = (
            cot[:, :, cols].reshape(256, 128).astype(F32) * fac[i : i + 1, :]
        ).astype(BF16)
    low_grad = nt(grad[...], up[...]).astype(BF16)
    low_grad_t = nt(up[...], grad[...]).astype(BF16)
    grad_a = nn(low_grad_t, tok[...])
    arrived(lows.at[fwd], l_recv.at[2 + fwd])
    arrived(lows.at[far], l_recv.at[2 + far])
    grad_b = nn(total(lows, 4).astype(BF16), grad[...])
    for q in range(16):
        r, b = q // 8, q % 8
        gb = grad_b[8 * r : 8 * r + 8] if b < 4 else grad_b[16 + 8 * r : 24 + 8 * r]
        gpart[q] = jnp.concatenate(
            [
                grad_a[16 * r : 16 * r + 16, 128 * b : 128 * b + 128],
                gb[:, 128 * b : 128 * b + 128],
                jnp.zeros((8, 128), F32),
            ],
            axis=0,
        ).astype(BF16)
    for k in range(1, 16):
        q = rem(p + k, 16)
        send(gpart.at[q], gplane.at[p], g1_send.at[k - 1], g1_recv.at[p], plane(q))
    gplane[p] = gpart[p]
    mag_tile.plane_send(mag_tile.core_sum())

    tg[...] = (
        sum(nn(grad[:, outputs(k)], weight[k].reshape(256, 1024)) for k in range(4))
        + nn(low_grad, dwn[...])
    ).astype(BF16)
    write(tg, tg_out, 0)

    collect(gplane, p, 16, g1_recv)
    gdepth[z] = total(gplane, 16)[0:24]
    spread(gdepth, z, 4, depth, g2_send, g2_recv)
    mag_tile.depth_send(mag_tile.plane_sum())

    for k in range(4):
        arrived(hop_in.at[k, 0], c_recv.at[4 + k])
        hop_out[k, 2] = (pair[k, fwd] + hop_in[k, 0].astype(F32)).astype(BF16)
        send(hop_out.at[k, 2], hop_in.at[k, 2], c_send.at[12 + k], c_recv.at[12 + k], tens(fwd))

    mag_tile.ring_send(mag_tile.depth_sum())
    collect(gdepth, z, 4, g2_recv)
    gfull[p] = jnp.concatenate([total(gdepth, 4), jnp.zeros((8, 128), F32)], axis=0).astype(BF16)
    spread(gfull, p, 16, plane, g4_send, g4_recv)
    mag_tile.ring_relay()

    for k in range(4):
        cols = outputs(k)
        arrived(hop_in.at[k, 1], c_recv.at[8 + k])
        arrived(hop_in.at[k, 2], c_recv.at[12 + k])
        summed = pair[k, h] + hop_in[k, 1].astype(F32) + hop_in[k, 2].astype(F32)
        proj[:, cols] = (summed * facrow[:, cols]).astype(BF16)
    write(proj, proj_out, 1)

    collect(gfull, p, 16, g4_recv)
    for q in range(16):
        r, b = q // 8, q % 8
        got = gfull[q].astype(F32) * scale
        da[16 * r : 16 * r + 16, 128 * b : 128 * b + 128] = got[0:16]
        lo = 128 * (b % 4)
        db[b // 4, 8 * r : 8 * r + 8, lo : lo + 128] = got[16:24]
    write(da, da_out, 2)
    write(db, db_out, 3)
    mgo[...] = mag_tile.ring_sum() / norm * scale
    write(mgo, mg_out, 4)

    for d in sends:
        d.wait_send()
    for w in writes:
        w.wait()


def finish(*refs):
    for src, dst in zip(refs[:5], refs[5:]):
        dst[...] = src[...]


def body(tokens, frozen, down_factor, up_factor, magnitude, key_value_gradient):
    scale = 1.0 / math.sqrt(tokens.shape[0] * lax.axis_size("dp"))
    dma = pltpu.SemaphoreType.DMA
    hbm = pl.BlockSpec(memory_space=pltpu.HBM)
    vmem = pl.BlockSpec(memory_space=pltpu.VMEM)
    outs = (
        jax.ShapeDtypeStruct((32, 1024), BF16),
        jax.ShapeDtypeStruct((256, 1024), BF16),
        jax.ShapeDtypeStruct((32, 1024), F32),
        jax.ShapeDtypeStruct((2, 16, 512), F32),
        jax.ShapeDtypeStruct((8, 128), F32),
    )
    results = pl.pallas_call(
        functools.partial(kernel, scale),
        out_shape=outs,
        in_specs=[hbm] * 6,
        out_specs=(hbm,) * 5,
        scratch_shapes=[
            pltpu.VMEM((32, 1024), BF16),
            pltpu.VMEM((256, 1024), BF16),
            pltpu.VMEM((32, 1024), F32),
            pltpu.VMEM((2, 16, 512), F32),
            pltpu.VMEM((8, 128), F32),
            pltpu.VMEM((256, 1024), BF16),
            pltpu.VMEM((32, 1024), BF16),
            pltpu.VMEM((8, 128), F32),
            pltpu.VMEM((4, 4, 4, 16, 1024), BF16),
            pltpu.VMEM((8, 32, 1024), BF16),
            pltpu.VMEM((32, 1024), BF16),
            pltpu.VMEM((4, 4, 2, 32, 256), F32),
            pltpu.VMEM((4, 4, 32, 256), F32),
            pltpu.VMEM((256, 1024), BF16),
            pltpu.VMEM((4, 4, 32, 256), BF16),
            pltpu.VMEM((4, 4, 32, 256), BF16),
            pltpu.VMEM((4, 3, 32, 256), BF16),
            pltpu.VMEM((4, 3, 32, 256), BF16),
            pltpu.VMEM((26, 8, 128), F32),
            pltpu.VMEM((26, 8, 128), F32),
            pltpu.VMEM((1, 1024), F32),
            pltpu.VMEM((2, 32, 256), F32),
            pltpu.VMEM((4, 32, 256), BF16),
            pltpu.VMEM((16, 32, 128), BF16),
            pltpu.VMEM((16, 32, 128), BF16),
            pltpu.VMEM((4, 24, 128), F32),
            pltpu.VMEM((16, 32, 128), BF16),
            dma((7,)),
            dma((5,)),
            dma((84,)),
            dma((84,)),
            dma((28,)),
            dma((28,)),
            dma((22,)),
            dma((26,)),
            dma((22,)),
            dma((26,)),
            dma((4,)),
            dma((6,)),
            dma((16,)),
            dma((16,)),
            dma((15,)),
            dma((3,)),
            dma((15,)),
            dma((16,)),
            dma((4,)),
            dma((16,)),
        ],
        compiler_params=pltpu.CompilerParams(
            collective_id=0, has_side_effects=True, vmem_limit_bytes=60 * 1024 * 1024
        ),
        cost_estimate=pl.CostEstimate(
            flops=1200000000, bytes_accessed=2000000, transcendentals=0
        ),
    )(
        tokens,
        frozen,
        down_factor,
        up_factor,
        magnitude.reshape(8, 128),
        key_value_gradient,
    )
    projected, token_gradient, grad_a, grad_b, grad_m = pl.pallas_call(
        finish,
        out_shape=outs,
        in_specs=[vmem] * 5,
        out_specs=(vmem,) * 5,
        compiler_params=pltpu.CompilerParams(vmem_limit_bytes=60 * 1024 * 1024),
    )(*results)
    return projected, token_gradient, grad_a, grad_b, grad_m.reshape(1024)


def solution(mesh):
    placed = (
        P("dp", "tensor"),
        P("dp", "tensor"),
        P(None, "tensor"),
        P(),
        P(),
        P(("dp", "tensor"), None),
    )
    return jax.shard_map(
        body,
        mesh=mesh,
        in_specs=placed,
        out_specs=(P(("dp", "tensor"), None), P("dp", "tensor"), P(None, "tensor"), P(), P()),
        check_vma=False,
    )
```

```python
import functools
import math

import jax
import jax.numpy as jnp
from jax import lax
from jax.experimental import pallas as pl
from jax.experimental.pallas import tpu as pltpu
from jax.sharding import PartitionSpec as P

stability_eps = 1e-06
MESH = pl.DeviceIdType.MESH
F32 = jnp.float32
BF16 = jnp.bfloat16
OFFSETS = (0, 3, 1, 2)


def nt(a, b):
    return lax.dot_general(a, b, (((1,), (1,)), ((), ())), preferred_element_type=F32)


def nn(a, b):
    return jnp.dot(a, b, preferred_element_type=F32)


def kernel(
    scale,
    tok_in,
    fro,
    dwn_in,
    upf,
    mag_in,
    kvg,
    proj_out,
    tg_out,
    da_out,
    db_out,
    mg_out,
    proj,
    tg,
    da,
    db,
    mgo,
    tok,
    dwn,
    mag,
    weight,
    cot,
    up,
    part,
    pair,
    grad,
    swap_out,
    swap_in,
    hop_out,
    hop_in,
    norms,
    mags,
    facrow,
    low_swap,
    lows,
    gpart,
    gplane,
    gdepth,
    gfull,
    met,
    in_sem,
    out_sem,
    f_send,
    f_recv,
    k_send,
    k_recv,
    n_send,
    n_recv,
    m_send,
    m_recv,
    l_send,
    l_recv,
    c_send,
    c_recv,
    g1_send,
    g2_send,
    g4_send,
    g1_recv,
    g2_recv,
    g4_recv,
):
    dp = lax.axis_index("dp")
    t = lax.axis_index("tensor")
    rem = lax.rem
    z, p = lax.div(dp, 16), rem(dp, 16)
    x, y = lax.div(p, 4), rem(p, 4)
    h, c = lax.div(t, 2), rem(t, 2)
    sib = (dp, h * 2 + 1 - c)
    fwd = rem(h + 1 + 2 * c, 4)
    bwd = rem(h + 3 + 2 * c, 4)
    far = rem(h + 2, 4)
    sends = []
    writes = []

    def at(zz, xx, yy):
        return ((zz * 4 + xx) * 4 + yy, t)

    def plane(q):
        return (z * 16 + q, t)

    def depth(q):
        return at(q, x, y)

    def column(q):
        return (rem(q, 4) * 16 + p, lax.div(q, 4) * 2 + c)

    def tens(hh):
        return (dp, hh * 2 + c)

    def send(src, dst, ssem, rsem, dev):
        d = pltpu.make_async_remote_copy(
            src_ref=src,
            dst_ref=dst,
            send_sem=ssem,
            recv_sem=rsem,
            device_id=dev,
            device_id_type=MESH,
        )
        d.start()
        sends.append(d)

    def arrived(dst, rsem):
        pltpu.make_async_remote_copy(
            src_ref=dst,
            dst_ref=dst,
            send_sem=f_send.at[0],
            recv_sem=rsem,
            device_id=sib,
            device_id_type=MESH,
        ).wait_recv()

    def spread(buf, own, n, peer, ssem, rsem, base=0, sbase=0):
        for k in range(1, n):
            send(
                buf.at[base + own], buf.at[base + own], ssem.at[sbase + k - 1],
                rsem.at[base + own], peer(rem(own + k, n)),
            )

    def collect(buf, own, n, rsem, base=0):
        for k in range(1, n):
            q = base + rem(own + k, n)
            arrived(buf.at[q], rsem.at[q])

    def total(buf, n, base=0):
        acc = buf[base].astype(F32)
        for i in range(1, n):
            acc = acc + buf[base + i].astype(F32)
        return acc

    def write(src, dst, i):
        w = pltpu.make_async_copy(src, dst, out_sem.at[i])
        w.start()
        writes.append(w)

    loads = [
        pltpu.make_async_copy(src, dst, in_sem.at[i])
        for i, (src, dst) in enumerate(
            (
                (fro, weight.at[0, x, y]),
                (dwn_in, dwn),
                (upf.at[0], up.at[pl.ds(0, 16), pl.ds(0, 512)]),
                (upf.at[1], up.at[pl.ds(16, 16), pl.ds(512, 512)]),
                (kvg, cot.at[t]),
                (tok_in, tok),
                (mag_in, mag),
            )
        )
    ]
    for load in loads:
        load.start()

    barrier = pltpu.get_barrier_semaphore()

    def greet(dev):
        pl.semaphore_signal(barrier, inc=1, device_id=dev, device_id_type=MESH)

    greet(tens(fwd))
    greet(tens(bwd))
    for k in range(1, 4):
        greet(depth(rem(z + k, 4)))
    for k in range(1, 16):
        greet(plane(rem(p + k, 16)))
    greet(sib)

    class Tile:
        def __init__(self, buf, ssem, rsem):
            self.buf, self.ssem, self.rsem = buf, ssem, rsem

        def core_send(self, value):
            self.buf[c] = value
            send(self.buf.at[c], self.buf.at[c], self.ssem.at[0], self.rsem.at[c], sib)

        def core_sum(self):
            arrived(self.buf.at[1 - c], self.rsem.at[1 - c])
            return self.buf[0] + self.buf[1]

        def ring_send(self, value):
            own = self.buf.at[2 + h]
            own[...] = value
            send(own, own, self.ssem.at[1], self.rsem.at[2 + h], tens(fwd))
            send(own, own, self.ssem.at[2], self.rsem.at[2 + h], tens(bwd))

        def ring_relay(self):
            got = self.buf.at[2 + bwd]
            arrived(got, self.rsem.at[2 + bwd])
            send(got, got, self.ssem.at[3], self.rsem.at[2 + bwd], tens(fwd))

        def ring_sum(self):
            arrived(self.buf.at[2 + fwd], self.rsem.at[2 + fwd])
            arrived(self.buf.at[2 + far], self.rsem.at[2 + far])
            return total(self.buf, 4, 2)

        def depth_send(self, value):
            self.buf[6 + z] = value
            spread(self.buf, z, 4, depth, self.ssem, self.rsem, 6, 4)

        def depth_sum(self):
            collect(self.buf, z, 4, self.rsem, 6)
            return total(self.buf, 4, 6)

        def plane_send(self, value):
            self.buf[10 + p] = value
            spread(self.buf, p, 16, plane, self.ssem, self.rsem, 10, 7)

        def column_send(self, value):
            self.buf[26 + h * 4 + z] = value
            spread(self.buf, h * 4 + z, 16, column, self.ssem, self.rsem, 26, 22)

        def column_sum(self):
            collect(self.buf, h * 4 + z, 16, self.rsem, 26)
            return total(self.buf, 16, 26)

        def plane_sum(self):
            collect(self.buf, p, 16, self.rsem, 10)
            return total(self.buf, 16, 10)

    norm_tile = Tile(norms, n_send, n_recv)
    mag_tile = Tile(mags, m_send, m_recv)

    up[0:16, 512:1024] = jnp.zeros((16, 512), BF16)
    up[16:32, 0:512] = jnp.zeros((16, 512), BF16)
    for load in loads:
        load.wait()
    row = lax.broadcasted_iota(jnp.int32, (16, 1024), 0)
    col = lax.broadcasted_iota(jnp.int32, (16, 1024), 1)
    pick = jnp.where(col == row + dp * 16, 1.0, 0.0).astype(BF16)
    mine = nt(pick, up[...]).astype(BF16)
    merged = weight[0, x, y].astype(F32) + nn(mine, dwn[...])
    squares = jnp.sum(merged * merged, axis=1, keepdims=True)
    row = lax.broadcasted_iota(jnp.int32, (16, 128), 0)
    col = lax.broadcasted_iota(jnp.int32, (16, 128), 1)
    line = jnp.sum(
        jnp.where(col == row + rem(dp, 8) * 16, squares, 0.0), axis=0, keepdims=True
    )
    row8 = lax.broadcasted_iota(jnp.int32, (8, 128), 0)
    own_squares = jnp.where(row8 == lax.div(dp, 8), line, 0.0)

    pl.semaphore_wait(barrier, 21)
    for hh in (fwd, bwd):
        pl.semaphore_signal(met.at[0], inc=1, device_id=tens(hh), device_id_type=MESH)

    own_rows = weight.at[0, x, y]
    for k in range(1, 4):
        send(own_rows, weight.at[4 - k, x, y], f_send.at[k], f_recv.at[4 - k],
             depth(rem(z + k, 4)))
    norm_tile.core_send(own_squares)

    pos = ((x, y), (y, x))

    def unit(half, grp, i, j):
        i, j = (i, j) if half == 0 else (j, i)
        return weight.at[pl.ds(2 * half, 2), i, j]

    def piece(half, grp, kind, i, j):
        i, j = (i, j) if half == 0 else (j, i)
        return weight.at[2 * half + kind, i, j]

    def peer(half, i, j):
        return at(z, i, j) if half == 0 else at(z, j, i)

    def sem(half, grp, step, kind):
        return 4 + ((half * 2 + grp) * 5 + step) * 4 + kind

    def pass_on(ref, s, dev):
        send(ref, ref, f_send.at[s], f_recv.at[s], dev)

    def first(grp):
        for kind, step in ((0, 1), (1, 3)):
            for half in range(2):
                i, j = pos[half]
                pass_on(unit(half, grp, i, j), sem(half, grp, 0, kind),
                        peer(half, rem(i + step, 4), j))

    def first_relay(grp):
        for kind, step in ((0, 1), (1, 3)):
            for half in range(2):
                i, j = pos[half]
                src = rem(i + 4 - step, 4)
                arrived(unit(half, grp, src, j), f_recv.at[sem(half, grp, 0, kind)])
                pass_on(piece(half, grp, kind, src, j), sem(half, grp, 0, 2 + kind),
                        peer(half, rem(i + step, 4), j))

    def first_done(grp):
        for kind in range(2):
            for half in range(2):
                i, j = pos[half]
                arrived(piece(half, grp, kind, rem(i + 2, 4), j),
                        f_recv.at[sem(half, grp, 0, 2 + kind)])

    def second(grp, g):
        for kind, step in ((0, 1), (1, 3)):
            for half in range(2):
                i, j = pos[half]
                u = rem(i + OFFSETS[g], 4)
                pass_on(unit(half, grp, u, j), sem(half, grp, 1 + g, kind),
                        peer(half, i, rem(j + step, 4)))

    def second_relay(grp, g):
        for kind, step in ((0, 1), (1, 3)):
            for half in range(2):
                i, j = pos[half]
                u, src = rem(i + OFFSETS[g], 4), rem(j + 4 - step, 4)
                arrived(unit(half, grp, u, src), f_recv.at[sem(half, grp, 1 + g, kind)])
                pass_on(piece(half, grp, kind, u, src), sem(half, grp, 1 + g, 2 + kind),
                        peer(half, i, rem(j + step, 4)))

    def second_done(grp, g):
        for kind in range(2):
            for half in range(2):
                i, j = pos[half]
                arrived(piece(half, grp, kind, rem(i + OFFSETS[g], 4), rem(j + 2, 4)),
                        f_recv.at[sem(half, grp, 1 + g, 2 + kind)])


    low_swap[c] = nt(dwn[...], tok[...])
    send(low_swap.at[c], low_swap.at[c], l_send.at[0], l_recv.at[c], sib)
    low = nt(tok[...], dwn[...])
    low_hi = low.astype(BF16)
    low_lo = (low - low_hi.astype(F32)).astype(BF16)

    norm_tile.ring_send(norm_tile.core_sum())

    def cot_at(hh, cc, i):
        return cot.at[hh * 2 + cc, :, pl.ds(512 * i, 512)]

    def cot_send(hh, kind, i, dev):
        ref = cot_at(hh, c, i)
        send(ref, ref, k_send.at[kind * 4 + i], k_recv.at[kind * 4 + i], dev)

    def cot_relay(i):
        arrived(cot_at(bwd, c, i), k_recv.at[i])
        cot_send(bwd, 2, i, tens(fwd))
        cot_send(bwd, 4, i, sib)

    for k in range(1, 4):
        arrived(weight.at[k, x, y], f_recv.at[k])
    first(1)
    second(1, 0)
    norm_tile.ring_relay()
    for i in range(2):
        cot_send(h, 0, i, tens(fwd))
    for i in range(2):
        cot_send(h, 1, i, tens(bwd))
    for i in range(2):
        cot_send(h, 3, i, sib)
    arrived(low_swap.at[1 - c], l_recv.at[1 - c])
    own_low = lows.at[h]
    own_low[...] = (low_swap[0] + low_swap[1]).astype(BF16)
    send(own_low, own_low, l_send.at[1], l_recv.at[2 + h], tens(fwd))
    send(own_low, own_low, l_send.at[2], l_recv.at[2 + h], tens(bwd))
    pl.semaphore_wait(met.at[0], 2)
    for hh in (fwd, bwd):
        pl.semaphore_signal(met.at[1], inc=1, device_id=tens(hh), device_id_type=MESH)
    first_relay(1)
    second(1, 1)
    second(1, 2)
    second_relay(1, 0)
    first_done(1)
    second(1, 3)
    norm_tile.depth_send(norm_tile.ring_sum())
    second_relay(1, 1)
    second_relay(1, 2)
    cot_relay(0)
    second_relay(1, 3)
    cot_relay(1)
    norm_tile.plane_send(norm_tile.depth_sum())
    for g in range(4):
        second_done(1, g)

    def outputs(k):
        return pl.ds(pl.multiple_of(rem(z + k, 4) * 256, 256), 256)

    for k in range(4):
        cols = outputs(k)
        rows = weight[k].reshape(256, 1024)
        out = nt(tok[...], rows) + nn(low_hi, up[:, cols]) + nn(low_lo, up[:, cols])
        part[k] = out.reshape(4, 2, 32, 256)
        swap_out[k] = part[k, :, 1 - c].astype(BF16)
        send(swap_out.at[k], swap_in.at[k], c_send.at[k], c_recv.at[k], sib)

    for i in range(2):
        arrived(cot_at(fwd, c, i), k_recv.at[4 + i])
        cot_send(fwd, 5, i, sib)

    arrived(lows.at[bwd], l_recv.at[2 + bwd])
    send(lows.at[bwd], lows.at[bwd], l_send.at[3], l_recv.at[2 + bwd], tens(fwd))

    for k in range(4):
        arrived(swap_in.at[k], c_recv.at[k])
        pair[k] = part[k, :, c] + swap_in[k].astype(F32)
        hop_out[k, 0] = pair[k, far].astype(BF16)
        send(hop_out.at[k, 0], hop_in.at[k, 0], c_send.at[4 + k], c_recv.at[4 + k], tens(fwd))
    for k in range(4):
        hop_out[k, 1] = pair[k, bwd].astype(BF16)
        send(hop_out.at[k, 1], hop_in.at[k, 1], c_send.at[8 + k], c_recv.at[8 + k], tens(bwd))

    for i in range(2):
        arrived(cot_at(far, c, i), k_recv.at[8 + i])
        cot_send(far, 6, i, sib)
    for i in range(2):
        arrived(cot_at(h, 1 - c, i), k_recv.at[12 + i])
        arrived(cot_at(fwd, 1 - c, i), k_recv.at[16 + i])
        arrived(cot_at(bwd, 1 - c, i), k_recv.at[20 + i])
        arrived(cot_at(far, 1 - c, i), k_recv.at[24 + i])

    mg = jnp.zeros((8, 128), F32)
    for k in range(4):
        m = jnp.sum(
            cot[:, :, outputs(k)].reshape(256, 256).astype(F32) * part[k].reshape(256, 256),
            axis=0,
            keepdims=True,
        )
        r = rem(z + k, 4) * 2
        mg = mg + jnp.where(row8 == r, m[:, 0:128], 0.0)
        mg = mg + jnp.where(row8 == r + 1, m[:, 128:256], 0.0)
    mag_tile.core_send(mg)

    pl.semaphore_wait(met.at[1], 2)
    mag_tile.plane_send(mag_tile.core_sum())
    def hop_relay(k):
        arrived(hop_in.at[k, 0], c_recv.at[4 + k])
        hop_out[k, 2] = (pair[k, fwd] + hop_in[k, 0].astype(F32)).astype(BF16)
        send(hop_out.at[k, 2], hop_in.at[k, 2], c_send.at[12 + k], c_recv.at[12 + k], tens(fwd))

    def hop_last(k):
        cols = outputs(k)
        arrived(hop_in.at[k, 1], c_recv.at[8 + k])
        arrived(hop_in.at[k, 2], c_recv.at[12 + k])
        summed = pair[k, h] + hop_in[k, 1].astype(F32) + hop_in[k, 2].astype(F32)
        proj[:, cols] = (summed * facrow[:, cols]).astype(BF16)

    norm = jnp.sqrt(norm_tile.plane_sum() + stability_eps)
    fac = mag[...] / norm
    for i in range(8):
        cols = pl.ds(i * 128, 128)
        facrow[:, cols] = fac[i : i + 1, :]
        grad[:, cols] = (
            cot[:, :, cols].reshape(256, 128).astype(F32) * fac[i : i + 1, :]
        ).astype(BF16)
    low_grad = nt(grad[...], up[...]).astype(BF16)
    low_grad_t = nt(up[...], grad[...]).astype(BF16)
    grad_a = nn(low_grad_t, tok[...])
    arrived(lows.at[fwd], l_recv.at[2 + fwd])
    arrived(lows.at[far], l_recv.at[2 + far])
    grad_b = nn(total(lows, 4).astype(BF16), grad[...])
    for q in range(16):
        r, b = q // 8, q % 8
        gb = grad_b[8 * r : 8 * r + 8] if b < 4 else grad_b[16 + 8 * r : 24 + 8 * r]
        gpart[q] = jnp.concatenate(
            [
                grad_a[16 * r : 16 * r + 16, 128 * b : 128 * b + 128],
                gb[:, 128 * b : 128 * b + 128],
                jnp.zeros((8, 128), F32),
            ],
            axis=0,
        ).astype(BF16)
    for k in range(1, 16):
        q = rem(p + k, 16)
        send(gpart.at[q], gplane.at[p], g1_send.at[k - 1], g1_recv.at[p], plane(q))
    gplane[p] = gpart[p]

    tg[...] = (
        sum(nn(grad[:, outputs(k)], weight[k].reshape(256, 1024)) for k in range(4))
        + nn(low_grad, dwn[...])
    ).astype(BF16)
    write(tg, tg_out, 0)

    mag_tile.column_send(mag_tile.plane_sum())
    hop_relay(0)
    hop_relay(1)
    collect(gplane, p, 16, g1_recv)
    gdepth[z] = total(gplane, 16)[0:24]
    spread(gdepth, z, 4, depth, g2_send, g2_recv)
    hop_relay(2)
    hop_relay(3)

    collect(gdepth, z, 4, g2_recv)
    gfull[p] = jnp.concatenate([total(gdepth, 4), jnp.zeros((8, 128), F32)], axis=0).astype(BF16)
    spread(gfull, p, 16, plane, g4_send, g4_recv)
    hop_last(0)
    hop_last(1)
    hop_last(2)
    hop_last(3)
    write(proj, proj_out, 1)

    collect(gfull, p, 16, g4_recv)
    for q in range(16):
        r, b = q // 8, q % 8
        got = gfull[q].astype(F32) * scale
        da[16 * r : 16 * r + 16, 128 * b : 128 * b + 128] = got[0:16]
        lo = 128 * (b % 4)
        db[b // 4, 8 * r : 8 * r + 8, lo : lo + 128] = got[16:24]
    write(da, da_out, 2)
    write(db, db_out, 3)
    mgo[...] = mag_tile.column_sum() / norm * scale
    write(mgo, mg_out, 4)

    for d in sends:
        d.wait_send()
    for w in writes:
        w.wait()


def finish(*refs):
    for src, dst in zip(refs[:5], refs[5:]):
        dst[...] = src[...]


def body(tokens, frozen, down_factor, up_factor, magnitude, key_value_gradient):
    scale = 1.0 / math.sqrt(tokens.shape[0] * lax.axis_size("dp"))
    dma = pltpu.SemaphoreType.DMA
    hbm = pl.BlockSpec(memory_space=pltpu.HBM)
    vmem = pl.BlockSpec(memory_space=pltpu.VMEM)
    outs = (
        jax.ShapeDtypeStruct((32, 1024), BF16),
        jax.ShapeDtypeStruct((256, 1024), BF16),
        jax.ShapeDtypeStruct((32, 1024), F32),
        jax.ShapeDtypeStruct((2, 16, 512), F32),
        jax.ShapeDtypeStruct((8, 128), F32),
    )
    results = pl.pallas_call(
        functools.partial(kernel, scale),
        out_shape=outs,
        in_specs=[hbm] * 6,
        out_specs=(hbm,) * 5,
        scratch_shapes=[
            pltpu.VMEM((32, 1024), BF16),
            pltpu.VMEM((256, 1024), BF16),
            pltpu.VMEM((32, 1024), F32),
            pltpu.VMEM((2, 16, 512), F32),
            pltpu.VMEM((8, 128), F32),
            pltpu.VMEM((256, 1024), BF16),
            pltpu.VMEM((32, 1024), BF16),
            pltpu.VMEM((8, 128), F32),
            pltpu.VMEM((4, 4, 4, 16, 1024), BF16),
            pltpu.VMEM((8, 32, 1024), BF16),
            pltpu.VMEM((32, 1024), BF16),
            pltpu.VMEM((4, 4, 2, 32, 256), F32),
            pltpu.VMEM((4, 4, 32, 256), F32),
            pltpu.VMEM((256, 1024), BF16),
            pltpu.VMEM((4, 4, 32, 256), BF16),
            pltpu.VMEM((4, 4, 32, 256), BF16),
            pltpu.VMEM((4, 3, 32, 256), BF16),
            pltpu.VMEM((4, 3, 32, 256), BF16),
            pltpu.VMEM((26, 8, 128), F32),
            pltpu.VMEM((42, 8, 128), F32),
            pltpu.VMEM((1, 1024), F32),
            pltpu.VMEM((2, 32, 256), F32),
            pltpu.VMEM((4, 32, 256), BF16),
            pltpu.VMEM((16, 32, 128), BF16),
            pltpu.VMEM((16, 32, 128), BF16),
            pltpu.VMEM((4, 24, 128), F32),
            pltpu.VMEM((16, 32, 128), BF16),
            pltpu.SemaphoreType.REGULAR((2,)),
            dma((7,)),
            dma((5,)),
            dma((84,)),
            dma((84,)),
            dma((28,)),
            dma((28,)),
            dma((22,)),
            dma((26,)),
            dma((37,)),
            dma((42,)),
            dma((4,)),
            dma((6,)),
            dma((16,)),
            dma((16,)),
            dma((15,)),
            dma((3,)),
            dma((15,)),
            dma((16,)),
            dma((4,)),
            dma((16,)),
        ],
        compiler_params=pltpu.CompilerParams(
            collective_id=0, has_side_effects=True, vmem_limit_bytes=60 * 1024 * 1024
        ),
        cost_estimate=pl.CostEstimate(
            flops=1200000000, bytes_accessed=2000000, transcendentals=0
        ),
    )(
        tokens,
        frozen,
        down_factor,
        up_factor,
        magnitude.reshape(8, 128),
        key_value_gradient,
    )
    projected, token_gradient, grad_a, grad_b, grad_m = pl.pallas_call(
        finish,
        out_shape=outs,
        in_specs=[vmem] * 5,
        out_specs=(vmem,) * 5,
        compiler_params=pltpu.CompilerParams(vmem_limit_bytes=60 * 1024 * 1024),
    )(*results)
    return projected, token_gradient, grad_a, grad_b, grad_m.reshape(1024)


def solution(mesh):
    placed = (
        P("dp", "tensor"),
        P("dp", "tensor"),
        P(None, "tensor"),
        P(),
        P(),
        P(("dp", "tensor"), None),
    )
    return jax.shard_map(
        body,
        mesh=mesh,
        in_specs=placed,
        out_specs=(P(("dp", "tensor"), None), P("dp", "tensor"), P(None, "tensor"), P(), P()),
        check_vma=False,
    )
```

```python
import functools
import math

import jax
import jax.numpy as jnp
from jax import lax
from jax.experimental import pallas as pl
from jax.experimental.pallas import tpu as pltpu
from jax.sharding import PartitionSpec as P

stability_eps = 1e-06
MESH = pl.DeviceIdType.MESH
F32 = jnp.float32
BF16 = jnp.bfloat16
OFFSETS = (0, 3, 1, 2)


def nt(a, b):
    return lax.dot_general(a, b, (((1,), (1,)), ((), ())), preferred_element_type=F32)


def nn(a, b):
    return jnp.dot(a, b, preferred_element_type=F32)


def kernel(
    scale,
    tok_in,
    fro,
    dwn_in,
    upf,
    mag_in,
    kvg,
    proj_out,
    tg_out,
    da_out,
    db_out,
    mg_out,
    proj,
    tg,
    da,
    db,
    mgo,
    tok,
    dwn,
    mag,
    weight,
    cot,
    up,
    part,
    pair,
    grad,
    swap_out,
    swap_in,
    hop_out,
    hop_in,
    norms,
    mags,
    facrow,
    low_swap,
    lows,
    gpart,
    gplane,
    gdepth,
    gfull,
    met,
    in_sem,
    out_sem,
    f_send,
    f_recv,
    k_send,
    k_recv,
    n_send,
    n_recv,
    m_send,
    m_recv,
    l_send,
    l_recv,
    c_send,
    c_recv,
    g1_send,
    g2_send,
    g4_send,
    g1_recv,
    g2_recv,
    g4_recv,
):
    dp = lax.axis_index("dp")
    t = lax.axis_index("tensor")
    rem = lax.rem
    z, p = lax.div(dp, 16), rem(dp, 16)
    x, y = lax.div(p, 4), rem(p, 4)
    h, c = lax.div(t, 2), rem(t, 2)
    sib = (dp, h * 2 + 1 - c)
    fwd = rem(h + 1 + 2 * c, 4)
    bwd = rem(h + 3 + 2 * c, 4)
    far = rem(h + 2, 4)
    sends = []
    writes = []

    def at(zz, xx, yy):
        return ((zz * 4 + xx) * 4 + yy, t)

    def plane(q):
        return (z * 16 + q, t)

    def depth(q):
        return at(q, x, y)

    def column(q):
        return (rem(q, 4) * 16 + p, lax.div(q, 4) * 2 + c)

    def tens(hh):
        return (dp, hh * 2 + c)

    def send(src, dst, ssem, rsem, dev):
        d = pltpu.make_async_remote_copy(
            src_ref=src,
            dst_ref=dst,
            send_sem=ssem,
            recv_sem=rsem,
            device_id=dev,
            device_id_type=MESH,
        )
        d.start()
        sends.append(d)

    def arrived(dst, rsem):
        pltpu.make_async_remote_copy(
            src_ref=dst,
            dst_ref=dst,
            send_sem=f_send.at[0],
            recv_sem=rsem,
            device_id=sib,
            device_id_type=MESH,
        ).wait_recv()

    def spread(buf, own, n, peer, ssem, rsem, base=0, sbase=0):
        for k in range(1, n):
            send(
                buf.at[base + own], buf.at[base + own], ssem.at[sbase + k - 1],
                rsem.at[base + own], peer(rem(own + k, n)),
            )

    def collect(buf, own, n, rsem, base=0):
        for k in range(1, n):
            q = base + rem(own + k, n)
            arrived(buf.at[q], rsem.at[q])

    def total(buf, n, base=0):
        acc = buf[base].astype(F32)
        for i in range(1, n):
            acc = acc + buf[base + i].astype(F32)
        return acc

    def write(src, dst, i):
        w = pltpu.make_async_copy(src, dst, out_sem.at[i])
        w.start()
        writes.append(w)

    loads = [
        pltpu.make_async_copy(src, dst, in_sem.at[i])
        for i, (src, dst) in enumerate(
            (
                (fro, weight.at[0, x, y]),
                (dwn_in, dwn),
                (upf.at[0], up.at[pl.ds(0, 16), pl.ds(0, 512)]),
                (upf.at[1], up.at[pl.ds(16, 16), pl.ds(512, 512)]),
                (kvg, cot.at[t]),
                (tok_in, tok),
                (mag_in, mag),
            )
        )
    ]
    for load in loads:
        load.start()

    barrier = pltpu.get_barrier_semaphore()

    def greet(dev):
        pl.semaphore_signal(barrier, inc=1, device_id=dev, device_id_type=MESH)

    greet(tens(fwd))
    greet(tens(bwd))
    for k in range(1, 4):
        greet(depth(rem(z + k, 4)))
    for k in range(1, 16):
        greet(plane(rem(p + k, 16)))
    greet(sib)

    class Tile:
        def __init__(self, buf, ssem, rsem):
            self.buf, self.ssem, self.rsem = buf, ssem, rsem

        def core_send(self, value):
            self.buf[c] = value
            send(self.buf.at[c], self.buf.at[c], self.ssem.at[0], self.rsem.at[c], sib)

        def core_sum(self):
            arrived(self.buf.at[1 - c], self.rsem.at[1 - c])
            return self.buf[0] + self.buf[1]

        def ring_send(self, value):
            own = self.buf.at[2 + h]
            own[...] = value
            send(own, own, self.ssem.at[1], self.rsem.at[2 + h], tens(fwd))
            send(own, own, self.ssem.at[2], self.rsem.at[2 + h], tens(bwd))

        def ring_relay(self):
            got = self.buf.at[2 + bwd]
            arrived(got, self.rsem.at[2 + bwd])
            send(got, got, self.ssem.at[3], self.rsem.at[2 + bwd], tens(fwd))

        def ring_sum(self):
            arrived(self.buf.at[2 + fwd], self.rsem.at[2 + fwd])
            arrived(self.buf.at[2 + far], self.rsem.at[2 + far])
            return total(self.buf, 4, 2)

        def depth_send(self, value):
            self.buf[6 + z] = value
            spread(self.buf, z, 4, depth, self.ssem, self.rsem, 6, 4)

        def depth_sum(self):
            collect(self.buf, z, 4, self.rsem, 6)
            return total(self.buf, 4, 6)

        def plane_send(self, value):
            self.buf[10 + p] = value
            spread(self.buf, p, 16, plane, self.ssem, self.rsem, 10, 7)

        def column_send(self, value):
            self.buf[26 + h * 4 + z] = value
            spread(self.buf, h * 4 + z, 16, column, self.ssem, self.rsem, 26, 22)

        def column_sum(self):
            collect(self.buf, h * 4 + z, 16, self.rsem, 26)
            return total(self.buf, 16, 26)

        def plane_sum(self):
            collect(self.buf, p, 16, self.rsem, 10)
            return total(self.buf, 16, 10)

    norm_tile = Tile(norms, n_send, n_recv)
    mag_tile = Tile(mags, m_send, m_recv)

    up[0:16, 512:1024] = jnp.zeros((16, 512), BF16)
    up[16:32, 0:512] = jnp.zeros((16, 512), BF16)
    for load in loads:
        load.wait()
    row = lax.broadcasted_iota(jnp.int32, (16, 1024), 0)
    col = lax.broadcasted_iota(jnp.int32, (16, 1024), 1)
    pick = jnp.where(col == row + dp * 16, 1.0, 0.0).astype(BF16)
    mine = nt(pick, up[...]).astype(BF16)
    merged = weight[0, x, y].astype(F32) + nn(mine, dwn[...])
    squares = jnp.sum(merged * merged, axis=1, keepdims=True)
    row = lax.broadcasted_iota(jnp.int32, (16, 128), 0)
    col = lax.broadcasted_iota(jnp.int32, (16, 128), 1)
    line = jnp.sum(
        jnp.where(col == row + rem(dp, 8) * 16, squares, 0.0), axis=0, keepdims=True
    )
    row8 = lax.broadcasted_iota(jnp.int32, (8, 128), 0)
    own_squares = jnp.where(row8 == lax.div(dp, 8), line, 0.0)

    pl.semaphore_wait(barrier, 21)
    for hh in (fwd, bwd):
        pl.semaphore_signal(met.at[0], inc=1, device_id=tens(hh), device_id_type=MESH)

    own_rows = weight.at[0, x, y]
    for k in range(1, 4):
        send(own_rows, weight.at[4 - k, x, y], f_send.at[k], f_recv.at[4 - k],
             depth(rem(z + k, 4)))
    norm_tile.core_send(own_squares)

    pos = ((x, y), (y, x))

    def unit(half, grp, i, j):
        i, j = (i, j) if half == 0 else (j, i)
        return weight.at[pl.ds(2 * half, 2), i, j]

    def piece(half, grp, kind, i, j):
        i, j = (i, j) if half == 0 else (j, i)
        return weight.at[2 * half + kind, i, j]

    def peer(half, i, j):
        return at(z, i, j) if half == 0 else at(z, j, i)

    def sem(half, grp, step, kind):
        return 4 + ((half * 2 + grp) * 5 + step) * 4 + kind

    def pass_on(ref, s, dev):
        send(ref, ref, f_send.at[s], f_recv.at[s], dev)

    def first(grp):
        for kind, step in ((0, 1), (1, 3)):
            for half in range(2):
                i, j = pos[half]
                pass_on(unit(half, grp, i, j), sem(half, grp, 0, kind),
                        peer(half, rem(i + step, 4), j))

    def first_relay(grp):
        for kind, step in ((0, 1), (1, 3)):
            for half in range(2):
                i, j = pos[half]
                src = rem(i + 4 - step, 4)
                arrived(unit(half, grp, src, j), f_recv.at[sem(half, grp, 0, kind)])
                pass_on(piece(half, grp, kind, src, j), sem(half, grp, 0, 2 + kind),
                        peer(half, rem(i + step, 4), j))

    def first_done(grp):
        for kind in range(2):
            for half in range(2):
                i, j = pos[half]
                arrived(piece(half, grp, kind, rem(i + 2, 4), j),
                        f_recv.at[sem(half, grp, 0, 2 + kind)])

    def second(grp, g):
        for kind, step in ((0, 1), (1, 3)):
            for half in range(2):
                i, j = pos[half]
                u = rem(i + OFFSETS[g], 4)
                pass_on(unit(half, grp, u, j), sem(half, grp, 1 + g, kind),
                        peer(half, i, rem(j + step, 4)))

    def second_relay(grp, g):
        for kind, step in ((0, 1), (1, 3)):
            for half in range(2):
                i, j = pos[half]
                u, src = rem(i + OFFSETS[g], 4), rem(j + 4 - step, 4)
                arrived(unit(half, grp, u, src), f_recv.at[sem(half, grp, 1 + g, kind)])
                pass_on(piece(half, grp, kind, u, src), sem(half, grp, 1 + g, 2 + kind),
                        peer(half, i, rem(j + step, 4)))

    def second_done(grp, g):
        for kind in range(2):
            for half in range(2):
                i, j = pos[half]
                arrived(piece(half, grp, kind, rem(i + OFFSETS[g], 4), rem(j + 2, 4)),
                        f_recv.at[sem(half, grp, 1 + g, 2 + kind)])


    low_swap[c] = nt(dwn[...], tok[...])
    send(low_swap.at[c], low_swap.at[c], l_send.at[0], l_recv.at[c], sib)
    low = nt(tok[...], dwn[...])
    low_hi = low.astype(BF16)
    low_lo = (low - low_hi.astype(F32)).astype(BF16)

    norm_tile.ring_send(norm_tile.core_sum())

    def cot_at(hh, cc, i):
        return cot.at[hh * 2 + cc, :, pl.ds(512 * i, 512)]

    def cot_send(hh, kind, i, dev):
        ref = cot_at(hh, c, i)
        send(ref, ref, k_send.at[kind * 4 + i], k_recv.at[kind * 4 + i], dev)

    def cot_relay(i):
        arrived(cot_at(bwd, c, i), k_recv.at[i])
        cot_send(bwd, 2, i, tens(fwd))
        cot_send(bwd, 4, i, sib)

    for k in range(1, 4):
        arrived(weight.at[k, x, y], f_recv.at[k])
    first(1)
    second(1, 0)
    norm_tile.ring_relay()
    for i in range(2):
        cot_send(h, 0, i, tens(fwd))
    for i in range(2):
        cot_send(h, 1, i, tens(bwd))
    for i in range(2):
        cot_send(h, 3, i, sib)
    arrived(low_swap.at[1 - c], l_recv.at[1 - c])
    own_low = lows.at[h]
    own_low[...] = (low_swap[0] + low_swap[1]).astype(BF16)
    send(own_low, own_low, l_send.at[1], l_recv.at[2 + h], tens(fwd))
    send(own_low, own_low, l_send.at[2], l_recv.at[2 + h], tens(bwd))
    pl.semaphore_wait(met.at[0], 2)
    for hh in (fwd, bwd):
        pl.semaphore_signal(met.at[1], inc=1, device_id=tens(hh), device_id_type=MESH)
    first_relay(1)
    second(1, 1)
    second(1, 2)
    second_relay(1, 0)
    first_done(1)
    second(1, 3)
    norm_tile.depth_send(norm_tile.ring_sum())
    cot_relay(0)
    second_relay(1, 1)
    second_relay(1, 2)
    cot_relay(1)
    second_relay(1, 3)
    norm_tile.plane_send(norm_tile.depth_sum())
    for g in range(4):
        second_done(1, g)

    def outputs(k):
        return pl.ds(pl.multiple_of(rem(z + k, 4) * 256, 256), 256)

    for k in range(4):
        cols = outputs(k)
        rows = weight[k].reshape(256, 1024)
        out = nt(tok[...], rows) + nn(low_hi, up[:, cols]) + nn(low_lo, up[:, cols])
        part[k] = out.reshape(4, 2, 32, 256)
        swap_out[k] = part[k, :, 1 - c].astype(BF16)
        if k % 2:
            two = pl.ds(k - 1, 2)
            send(swap_out.at[two], swap_in.at[two], c_send.at[k // 2], c_recv.at[k // 2], sib)

    for i in range(2):
        arrived(cot_at(fwd, c, i), k_recv.at[4 + i])
        cot_send(fwd, 5, i, sib)

    arrived(lows.at[bwd], l_recv.at[2 + bwd])
    send(lows.at[bwd], lows.at[bwd], l_send.at[3], l_recv.at[2 + bwd], tens(fwd))

    def hop_send(m, kind, dev):
        two = pl.ds(2 * m, 2)
        s = 4 * (kind + 1) + m
        send(hop_out.at[two, kind], hop_in.at[two, kind], c_send.at[s], c_recv.at[s], dev)

    def hop_arrived(m, kind):
        arrived(hop_in.at[pl.ds(2 * m, 2), kind], c_recv.at[4 * (kind + 1) + m])

    for m in range(2):
        arrived(swap_in.at[pl.ds(2 * m, 2)], c_recv.at[m])
        for k in (2 * m, 2 * m + 1):
            pair[k] = part[k, :, c] + swap_in[k].astype(F32)
            hop_out[k, 0] = pair[k, far].astype(BF16)
        hop_send(m, 0, tens(fwd))
    for m in range(2):
        for k in (2 * m, 2 * m + 1):
            hop_out[k, 1] = pair[k, bwd].astype(BF16)
        hop_send(m, 1, tens(bwd))

    for i in range(2):
        arrived(cot_at(far, c, i), k_recv.at[8 + i])
        cot_send(far, 6, i, sib)
    for i in range(2):
        arrived(cot_at(h, 1 - c, i), k_recv.at[12 + i])
        arrived(cot_at(fwd, 1 - c, i), k_recv.at[16 + i])
        arrived(cot_at(bwd, 1 - c, i), k_recv.at[20 + i])
        arrived(cot_at(far, 1 - c, i), k_recv.at[24 + i])

    mg = jnp.zeros((8, 128), F32)
    for k in range(4):
        m = jnp.sum(
            cot[:, :, outputs(k)].reshape(256, 256).astype(F32) * part[k].reshape(256, 256),
            axis=0,
            keepdims=True,
        )
        r = rem(z + k, 4) * 2
        mg = mg + jnp.where(row8 == r, m[:, 0:128], 0.0)
        mg = mg + jnp.where(row8 == r + 1, m[:, 128:256], 0.0)
    mag_tile.core_send(mg)

    pl.semaphore_wait(met.at[1], 2)
    mag_tile.plane_send(mag_tile.core_sum())
    def hop_relay(m):
        hop_arrived(m, 0)
        for k in (2 * m, 2 * m + 1):
            hop_out[k, 2] = (pair[k, fwd] + hop_in[k, 0].astype(F32)).astype(BF16)
        hop_send(m, 2, tens(fwd))

    def hop_last(k):
        cols = outputs(k)
        if k % 2 == 0:
            hop_arrived(k // 2, 1)
            hop_arrived(k // 2, 2)
        summed = pair[k, h] + hop_in[k, 1].astype(F32) + hop_in[k, 2].astype(F32)
        proj[:, cols] = (summed * facrow[:, cols]).astype(BF16)

    norm = jnp.sqrt(norm_tile.plane_sum() + stability_eps)
    fac = mag[...] / norm
    for i in range(8):
        cols = pl.ds(i * 128, 128)
        facrow[:, cols] = fac[i : i + 1, :]
        grad[:, cols] = (
            cot[:, :, cols].reshape(256, 128).astype(F32) * fac[i : i + 1, :]
        ).astype(BF16)
    low_grad = nt(grad[...], up[...]).astype(BF16)
    low_grad_t = nt(up[...], grad[...]).astype(BF16)
    grad_a = nn(low_grad_t, tok[...])
    arrived(lows.at[fwd], l_recv.at[2 + fwd])
    arrived(lows.at[far], l_recv.at[2 + far])
    grad_b = nn(total(lows, 4).astype(BF16), grad[...])
    for q in range(16):
        r, b = q // 8, q % 8
        gb = grad_b[8 * r : 8 * r + 8] if b < 4 else grad_b[16 + 8 * r : 24 + 8 * r]
        gpart[q] = jnp.concatenate(
            [
                grad_a[16 * r : 16 * r + 16, 128 * b : 128 * b + 128],
                gb[:, 128 * b : 128 * b + 128],
                jnp.zeros((8, 128), F32),
            ],
            axis=0,
        ).astype(BF16)
    for k in range(1, 16):
        q = rem(p + k, 16)
        send(gpart.at[q], gplane.at[p], g1_send.at[k - 1], g1_recv.at[p], plane(q))
    gplane[p] = gpart[p]

    tg[...] = (
        sum(nn(grad[:, outputs(k)], weight[k].reshape(256, 1024)) for k in range(4))
        + nn(low_grad, dwn[...])
    ).astype(BF16)
    write(tg, tg_out, 0)

    mag_tile.column_send(mag_tile.plane_sum())
    hop_relay(0)
    collect(gplane, p, 16, g1_recv)
    gdepth[z] = total(gplane, 16)[0:24]
    spread(gdepth, z, 4, depth, g2_send, g2_recv)
    hop_relay(1)

    collect(gdepth, z, 4, g2_recv)
    gfull[p] = jnp.concatenate([total(gdepth, 4), jnp.zeros((8, 128), F32)], axis=0).astype(BF16)
    spread(gfull, p, 16, plane, g4_send, g4_recv)
    hop_last(0)
    hop_last(1)
    hop_last(2)
    hop_last(3)
    write(proj, proj_out, 1)

    collect(gfull, p, 16, g4_recv)
    for q in range(16):
        r, b = q // 8, q % 8
        got = gfull[q].astype(F32) * scale
        da[16 * r : 16 * r + 16, 128 * b : 128 * b + 128] = got[0:16]
        lo = 128 * (b % 4)
        db[b // 4, 8 * r : 8 * r + 8, lo : lo + 128] = got[16:24]
    write(da, da_out, 2)
    write(db, db_out, 3)
    mgo[...] = mag_tile.column_sum() / norm * scale
    write(mgo, mg_out, 4)

    for d in sends:
        d.wait_send()
    for w in writes:
        w.wait()


def finish(*refs):
    for src, dst in zip(refs[:5], refs[5:]):
        dst[...] = src[...]


def body(tokens, frozen, down_factor, up_factor, magnitude, key_value_gradient):
    scale = 1.0 / math.sqrt(tokens.shape[0] * lax.axis_size("dp"))
    dma = pltpu.SemaphoreType.DMA
    hbm = pl.BlockSpec(memory_space=pltpu.HBM)
    vmem = pl.BlockSpec(memory_space=pltpu.VMEM)
    outs = (
        jax.ShapeDtypeStruct((32, 1024), BF16),
        jax.ShapeDtypeStruct((256, 1024), BF16),
        jax.ShapeDtypeStruct((32, 1024), F32),
        jax.ShapeDtypeStruct((2, 16, 512), F32),
        jax.ShapeDtypeStruct((8, 128), F32),
    )
    results = pl.pallas_call(
        functools.partial(kernel, scale),
        out_shape=outs,
        in_specs=[hbm] * 6,
        out_specs=(hbm,) * 5,
        scratch_shapes=[
            pltpu.VMEM((32, 1024), BF16),
            pltpu.VMEM((256, 1024), BF16),
            pltpu.VMEM((32, 1024), F32),
            pltpu.VMEM((2, 16, 512), F32),
            pltpu.VMEM((8, 128), F32),
            pltpu.VMEM((256, 1024), BF16),
            pltpu.VMEM((32, 1024), BF16),
            pltpu.VMEM((8, 128), F32),
            pltpu.VMEM((4, 4, 4, 16, 1024), BF16),
            pltpu.VMEM((8, 32, 1024), BF16),
            pltpu.VMEM((32, 1024), BF16),
            pltpu.VMEM((4, 4, 2, 32, 256), F32),
            pltpu.VMEM((4, 4, 32, 256), F32),
            pltpu.VMEM((256, 1024), BF16),
            pltpu.VMEM((4, 4, 32, 256), BF16),
            pltpu.VMEM((4, 4, 32, 256), BF16),
            pltpu.VMEM((4, 3, 32, 256), BF16),
            pltpu.VMEM((4, 3, 32, 256), BF16),
            pltpu.VMEM((26, 8, 128), F32),
            pltpu.VMEM((42, 8, 128), F32),
            pltpu.VMEM((1, 1024), F32),
            pltpu.VMEM((2, 32, 256), F32),
            pltpu.VMEM((4, 32, 256), BF16),
            pltpu.VMEM((16, 32, 128), BF16),
            pltpu.VMEM((16, 32, 128), BF16),
            pltpu.VMEM((4, 24, 128), F32),
            pltpu.VMEM((16, 32, 128), BF16),
            pltpu.SemaphoreType.REGULAR((2,)),
            dma((7,)),
            dma((5,)),
            dma((84,)),
            dma((84,)),
            dma((28,)),
            dma((28,)),
            dma((22,)),
            dma((26,)),
            dma((37,)),
            dma((42,)),
            dma((4,)),
            dma((6,)),
            dma((16,)),
            dma((16,)),
            dma((15,)),
            dma((3,)),
            dma((15,)),
            dma((16,)),
            dma((4,)),
            dma((16,)),
        ],
        compiler_params=pltpu.CompilerParams(
            collective_id=0, has_side_effects=True, vmem_limit_bytes=60 * 1024 * 1024
        ),
        cost_estimate=pl.CostEstimate(
            flops=1200000000, bytes_accessed=2000000, transcendentals=0
        ),
    )(
        tokens,
        frozen,
        down_factor,
        up_factor,
        magnitude.reshape(8, 128),
        key_value_gradient,
    )
    projected, token_gradient, grad_a, grad_b, grad_m = pl.pallas_call(
        finish,
        out_shape=outs,
        in_specs=[vmem] * 5,
        out_specs=(vmem,) * 5,
        compiler_params=pltpu.CompilerParams(vmem_limit_bytes=60 * 1024 * 1024),
    )(*results)
    return projected, token_gradient, grad_a, grad_b, grad_m.reshape(1024)


def solution(mesh):
    placed = (
        P("dp", "tensor"),
        P("dp", "tensor"),
        P(None, "tensor"),
        P(),
        P(),
        P(("dp", "tensor"), None),
    )
    return jax.shard_map(
        body,
        mesh=mesh,
        in_specs=placed,
        out_specs=(P(("dp", "tensor"), None), P("dp", "tensor"), P(None, "tensor"), P(), P()),
        check_vma=False,
    )
```
